32 devices in a mesh: bis: 4 (over x, core), slab: 8 (over z, y).
Axes of the slice: x: 2, y: 2, z: 4, core: 2. Of those that a mesh axis runs over, the one named last changes fastest.
Arguments:
- positions: float32 [3, 32, 32768], P(None, None, ('bis', 'slab')), may hold values from 0 to 1
- forces: float32 [3, 32, 32768], P(None, None, ('bis', 'slab')), may hold values from -6 to 6
- self_blocks: bfloat16 [96, 96, 32768], P(None, None, ('bis', 'slab')), may hold values from -0.625 to 0.625
- cut_lists: int32 [3, 8192], P(None, ('bis', 'slab')), may hold values from 0 to 1023, as said below
- pair_tiles: int32 [4, 8192], P(None, ('bis', 'slab')), may hold values from -1 to 8191, as said below
Outputs:
- velocity: float32 [3, 32, 32768], P(None, None, ('bis', 'slab'))
The draws below stay inside these ranges and needn't reach their ends.
Inputs may be any that keep to these rules, and one draw needn't show every extreme that they name: `cut_lists`: for each level and device the 256 entries are distinct slots of that device. `pair_tiles`: tile id (b * 8 + s) * 256 + t is tile t of device (b, s). Every entry of a device's targets is -1 or a tile of the device with the same slab index and a bis index one lower, equal or one higher, cyclically; each device's entries name exactly 64 distinct tiles of each of its two neighbouring devices.
All inputs are finite; a program needn't handle non-finite values.
Results may differ from the reference program's by a relative error of at most 0.0003.
Values sent between devices are 32-bit elements; how exact they have to be, the bound alone decides.
A program may use at most 128 MiB of HBM per device.

```python
import math
import jax
import jax.numpy as jnp
from jax import lax

NODES = 32
TILE = 4
NB = 4
F_DEV = 1024
TT = 256
K = 256
REQ = 64
LEVELS = 3
NF = 32768
N_BIS = 4
N_SLAB = 8


def draw_cut_lists(key, part):
    row_total = LEVELS * N_BIS * N_SLAB
    scores = jax.random.randint(key, (row_total, F_DEV), 0, 2 ** 19) * F_DEV + jnp.arange(F_DEV, dtype=jnp.int32)[None, :]
    chosen = lax.top_k(scores, K)[1]
    return chosen.astype(jnp.int32).reshape(LEVELS, N_BIS * N_SLAB * K)


def draw_pair_tiles(key, part):
    device_total = N_BIS * N_SLAB
    entry_total = NB * TT
    key_list = jax.random.split(jax.random.fold_in(key, 7), 7)
    column_ids = jnp.arange(TT, dtype=jnp.int32)[None, :]
    left_pick = lax.top_k(jax.random.randint(key_list[0], (device_total, TT), 0, 2 ** 19) * TT + column_ids, REQ)[1]
    right_pick = lax.top_k(jax.random.randint(key_list[1], (device_total, TT), 0, 2 ** 19) * TT + column_ids, REQ)[1]
    linear = jnp.arange(device_total, dtype=jnp.int32)
    bis_row = linear // N_SLAB
    slab_col = linear % N_SLAB
    left_dev = (bis_row + N_BIS - 1) % N_BIS * N_SLAB + slab_col
    right_dev = (bis_row + 1) % N_BIS * N_SLAB + slab_col
    left_ids = left_dev[:, None] * TT + left_pick
    right_ids = right_dev[:, None] * TT + right_pick
    kind_draw = jax.random.randint(key_list[2], (device_total, entry_total), 0, 4)
    from_left = jnp.take_along_axis(left_ids, jax.random.randint(key_list[3], (device_total, entry_total), 0, REQ), axis=1)
    from_right = jnp.take_along_axis(right_ids, jax.random.randint(key_list[4], (device_total, entry_total), 0, REQ), axis=1)
    own_ids = linear[:, None] * TT + jax.random.randint(key_list[5], (device_total, entry_total), 0, TT)
    filler = jnp.where(kind_draw == 0, own_ids, jnp.where(kind_draw == 1, from_left, jnp.where(kind_draw == 2, from_right, -1)))
    slot_ids = jnp.arange(entry_total, dtype=jnp.int32)
    forced_left = jnp.take(left_ids, jnp.minimum(slot_ids, REQ - 1), axis=1)
    forced_right = jnp.take(right_ids, jnp.clip(slot_ids - REQ, 0, REQ - 1), axis=1)
    forced = jnp.where(slot_ids[None, :] < REQ, forced_left, jnp.where(slot_ids[None, :] < 2 * REQ, forced_right, filler))
    shuffle = lax.top_k(jax.random.randint(key_list[6], (device_total, entry_total), 0, 2 ** 19) * entry_total + slot_ids[None, :], entry_total)[1]
    shuffled = jnp.take_along_axis(forced, shuffle, axis=1)
    return shuffled.reshape(device_total, NB, TT).transpose(1, 0, 2).reshape(NB, device_total * TT).astype(jnp.int32)


def block_scale(own_key, dims, shards, low, top_value):
    factor_of, own = 1.0, jax.random.fold_in(own_key, 6)
    for dim, parts in shards:
        draws = jnp.exp(jax.random.uniform(jax.random.fold_in(own, dim), (parts,), jnp.float32, low / len(shards), top_value / len(shards)))
        factor_of = factor_of * jnp.repeat(draws, dims[dim] // parts).reshape([-1 if axis == dim else 1 for axis in range(len(dims))])
    return factor_of


def normal_values(rng, extent, spread, reach, pieces=(), kind=jnp.bfloat16):
    drawn = spread * jax.random.normal(rng, extent, jnp.float32)
    if pieces:
        drawn = drawn * block_scale(rng, extent, pieces, -0.22, 0.18)
    return jnp.clip(drawn, -reach, reach).astype(kind)


def setup_inputs(seed: int = 0) -> dict:
    key_of = jax.random.split(jax.random.key(seed), 6)
    return {
        "positions": jnp.clip(1.0 * jax.random.uniform(key_of[0], (3, NODES, NF), jnp.float32) ** block_scale(key_of[0], (3, NODES, NF), ((2, 32),), -0.2, 0.2), 0.0, 1.0),
        "forces": normal_values(key_of[1], (3, NODES, NF), 1.0, 6.0, ((2, 32),), jnp.float32),
        "self_blocks": normal_values(key_of[2], (3 * NODES, 3 * NODES, NF), (3 * NODES) ** -0.5, 0.625, ((2, 32),)),
        "cut_lists": draw_cut_lists(jax.random.fold_in(key_of[5], 71), 0),
        "pair_tiles": draw_pair_tiles(jax.random.fold_in(key_of[5], 71), 0),
    }


blob_eps2 = 0.0025
stokes_scale = 1.0 / (8.0 * math.pi)

def stokeslet(targets, sources, pushes, weights):
    offset_vec = targets[:, None, :, :, None] - sources[:, :, :, None, :]
    radius2 = lax.optimization_barrier(jnp.sum(offset_vec * offset_vec, axis=0)) + blob_eps2
    inverse = lax.rsqrt(radius2) * weights[:, :, None, None]
    inverse3 = inverse * inverse * inverse
    dot_force = lax.optimization_barrier(jnp.sum(offset_vec * pushes[:, :, :, None, :], axis=0))
    summed = lax.optimization_barrier(jnp.sum(pushes[:, :, :, None, :] * inverse[None] + offset_vec * (dot_force * inverse3)[None], axis=(1, 4)))
    return summed * stokes_scale

def to_tiles(values, count):
    return values.reshape(3, NODES, count, TILE).transpose(0, 2, 3, 1).reshape(3, count, TILE * NODES)

def from_tiles(values, count):
    return values.reshape(3, count, TILE, NODES).transpose(0, 3, 1, 2).reshape(3, NODES, count * TILE)

def reference(positions, forces, self_blocks, cut_lists, pair_tiles):
    devices = N_BIS * N_SLAB
    fibre_total = devices * F_DEV
    unknowns = 3 * NODES
    anchor = jnp.arange(fibre_total, dtype=jnp.int32).reshape(N_BIS, N_SLAB, F_DEV)
    device_base = (jnp.arange(devices, dtype=jnp.int32) * F_DEV).reshape(N_BIS, N_SLAB, 1)
    for section_no in range(LEVELS):
        spacing = N_SLAB // 2 ** (section_no + 1)
        chosen = cut_lists[section_no].reshape(N_BIS, N_SLAB, K)
        handed = jnp.take_along_axis(anchor, chosen, axis=2)
        handed = handed.reshape(N_BIS, N_SLAB // (2 * spacing), 2, spacing, K)[:, :, ::-1].reshape(-1)
        target_slots = (device_base + chosen).reshape(-1)
        anchor = anchor.reshape(-1).at[target_slots].set(handed).reshape(N_BIS, N_SLAB, F_DEV)
    anchor = anchor.reshape(-1)
    flat_forces = forces.reshape(unknowns, fibre_total)

    def self_apply(block_no):
        first_col = block_no * F_DEV
        blocks = lax.dynamic_slice_in_dim(self_blocks, first_col, F_DEV, axis=2).astype(jnp.float32)
        pushes = lax.dynamic_slice_in_dim(flat_forces, first_col, F_DEV, axis=1)
        return lax.optimization_barrier(jnp.sum(blocks * pushes[None], axis=1))
    own_velocity = lax.map(self_apply, jnp.arange(devices, dtype=jnp.int32))
    own_velocity = own_velocity.transpose(1, 0, 2).reshape(unknowns, fibre_total)
    self_velocity = jnp.take(own_velocity, anchor, axis=1)
    moved_positions = jnp.take(positions.reshape(unknowns, fibre_total), anchor, axis=1)
    moved_forces = jnp.take(flat_forces, anchor, axis=1)
    tile_total = fibre_total // TILE
    tile_pos = to_tiles(moved_positions, tile_total)
    tile_force = to_tiles(moved_forces, tile_total)
    block_len = math.gcd(tile_total, 64)

    def stokes_block(block_no):
        first_tile = block_no * block_len
        listed = lax.dynamic_slice_in_dim(pair_tiles, first_tile, block_len, axis=1)
        weights = (listed >= 0).astype(jnp.float32)
        safe_ids = jnp.maximum(listed, 0).reshape(-1)
        sources = jnp.take(tile_pos, safe_ids, axis=1).reshape(3, NB, block_len, TILE * NODES)
        pushes = jnp.take(tile_force, safe_ids, axis=1).reshape(3, NB, block_len, TILE * NODES)
        targets = lax.dynamic_slice_in_dim(tile_pos, first_tile, block_len, axis=1)
        return stokeslet(targets, sources, pushes, weights)
    swept = lax.map(stokes_block, jnp.arange(tile_total // block_len, dtype=jnp.int32))
    stokes_velocity = swept.transpose(1, 0, 2, 3).reshape(3, tile_total, TILE * NODES)
    return self_velocity.reshape(3, NODES, fibre_total) + from_tiles(stokes_velocity, tile_total)
```

```python
import math, functools
import jax, jax.numpy as jnp
from jax import lax
from jax.experimental import pallas as pl
from jax.experimental.pallas import tpu as pltpu
from jax.sharding import PartitionSpec as P

NODES = 32
TILE = 4


blob_eps2 = 0.0025
stokes_scale = 1.0 / (8.0 * math.pi)


def pieces(t):
    h1 = t.astype(jnp.bfloat16).astype(jnp.float32)
    r = t - h1
    h2 = r.astype(jnp.bfloat16).astype(jnp.float32)
    h3 = (r - h2).astype(jnp.bfloat16).astype(jnp.float32)
    return h1, h2, h3


def target_features(t):
    h1, h2, h3 = pieces(t)
    row = lax.broadcasted_iota(jnp.int32, (8, 128), 0)
    zero = jnp.zeros((8, 128), jnp.float32)

    def near(h, unit):
        return jnp.where(row < 3, -2.0 * h, jnp.where(row == 6, unit, 0.0))

    def push(h, unit):
        return jnp.where(
            (row >= 3) & (row < 6), pltpu.roll(h, 3, axis=0), jnp.where(row == 7, unit, 0.0)
        )

    norm = jnp.broadcast_to(t[6:7] + blob_eps2, (8, 128))
    e1, e2, e3 = pieces(norm)
    own = jnp.where(row == 0, e1, jnp.where(row == 1, e2, jnp.where(row == 2, e3, 0.0)))
    order = [(h1, 1.0), (h1, 1.0), (h2, 0.0), (h2, 0.0), (h1, 1.0), (h3, 0.0)]
    left = jnp.concatenate([near(h, u) for h, u in order] + [own, zero], axis=0)
    right = jnp.concatenate([push(h, u) for h, u in order] + [zero, zero], axis=0)
    return jnp.concatenate([left, right], axis=1).astype(jnp.bfloat16)


def stokes_kernel(entries, look, ext, out, packed, qp0, qp1, acc0, acc1):
    count = out.shape[1]
    total = ext.shape[0]

    @pl.loop(0, total // 8)
    def _(i):
        first = pl.multiple_of(i * 8, 8)
        h1, h2, h3 = pieces(ext[pl.ds(first, 8)])
        packed[pl.ds(first, 8)] = jnp.concatenate([h1, h2, h3, h1], axis=1).astype(jnp.bfloat16)

    ones16 = jnp.ones((16, 128), jnp.bfloat16)

    def products(g, qp):
        feats = target_features(ext[g])
        for n in range(0, entries, 2):
            side = []
            for k in (n, n + 1):
                e = look[k, g]
                low = packed[e, 0:16]
                side.append(jnp.concatenate([low, low, packed[e, 16:32], ones16], axis=0))
            sources = jnp.concatenate(side, axis=1)
            qp[:, n * 128 : (n + 2) * 128] = lax.dot_general(
                feats, sources, (((0,), (0,)), ((), ())), preferred_element_type=jnp.float32
            )

    def sweep(g, qp, acc):
        ys, fs = [], []
        for n in range(entries):
            e = look[n, g]
            ys.append([jnp.broadcast_to(ext[e, i : i + 1], (8, 128)) for i in range(3)])
            fs.append([jnp.broadcast_to(ext[e, i + 3 : i + 4], (8, 128)) for i in range(3)])
        for c in range(16):
            tot = None
            for n in range(entries):
                q = qp[c * 8 : c * 8 + 8, n * 128 : n * 128 + 128]
                p = qp[128 + c * 8 : 136 + c * 8, n * 128 : n * 128 + 128]
                w = lax.rsqrt(q)
                s = p * (w * w) * w
                part = [w * fs[n][i] - s * ys[n][i] for i in range(3)] + [s]
                tot = part if tot is None else [a + b for a, b in zip(tot, part)]
            for i in range(4):
                high = tot[i].astype(jnp.bfloat16).astype(jnp.float32)
                acc[i * 128 + c * 8 : i * 128 + c * 8 + 8, 0:128] = tot[i]

    def finish(g, acc):
        a = acc[...]
        high = a.astype(jnp.bfloat16)
        low = (a - high.astype(jnp.float32)).astype(jnp.bfloat16)
        sums = lax.dot_general(
            jnp.ones((8, 256), jnp.bfloat16), jnp.concatenate([high, low], axis=1),
            (((1,), (1,)), ((), ())), preferred_element_type=jnp.float32,
        )
        t = ext[g]
        for i in range(3):
            out[i, pl.ds(g, 1)] = stokes_scale * (
                sums[0:1, i * 128 : i * 128 + 128] + t[i : i + 1] * sums[0:1, 384:512]
            )

    products(0, qp0)

    @pl.loop(0, count // 2)
    def _(h):
        g = h * 2
        products(g + 1, qp1)
        sweep(g, qp0, acc0)
        products(jnp.minimum(g + 2, count - 1), qp0)
        finish(g, acc0)
        sweep(g + 1, qp1, acc1)
        finish(g + 1, acc1)


def stokes_tiles(ext, look):
    entries, count = look.shape
    total = ext.shape[0]
    return pl.pallas_call(
        functools.partial(stokes_kernel, entries),
        out_shape=jax.ShapeDtypeStruct((3, count, 128), jnp.float32),
        in_specs=[pl.BlockSpec(memory_space=pltpu.SMEM), pl.BlockSpec(memory_space=pltpu.VMEM)],
        out_specs=pl.BlockSpec(memory_space=pltpu.VMEM),
        scratch_shapes=[
            pltpu.VMEM((total, 32, 128), jnp.bfloat16),
            pltpu.VMEM((256, entries * 128), jnp.float32),
            pltpu.VMEM((256, entries * 128), jnp.float32),
            pltpu.VMEM((512, 128), jnp.float32),
            pltpu.VMEM((512, 128), jnp.float32),
        ],
        compiler_params=pltpu.CompilerParams(vmem_limit_bytes=48 * 2**20),
        cost_estimate=pl.CostEstimate(flops=400_000_000, bytes_accessed=2_000_000, transcendentals=0),
    )(look, ext)


def swapped(block, axis, distance):
    count = lax.axis_size(axis)
    route = []
    for low in range(count):
        high = low | 1 << distance
        if high != low and high < count:
            route += [(low, high), (high, low)]
    return lax.ppermute(block, axis, route)


def with_halo(block, sides, width):
    for axis, dim in sides:
        count = lax.axis_size(axis)
        forward = [(i, i + 1) for i in range(count - 1)]
        forward.append((count - 1, 0))
        backward = [(target, source) for source, target in forward]
        low = lax.ppermute(
            lax.slice_in_dim(block, block.shape[dim] - width, None, axis=dim), axis, forward
        )
        high = lax.ppermute(lax.slice_in_dim(block, 0, width, axis=dim), axis, backward)
        block = jnp.concatenate([low, block, high], axis=dim)
    return block


def rows_to_tiles(rows, count):
    return rows.reshape(count, TILE, 3, NODES).transpose(2, 0, 1, 3).reshape(3, count, TILE * NODES)


def from_tiles(values, count):
    return (
        values.reshape(3, count, TILE, NODES).transpose(0, 3, 1, 2).reshape(3, NODES, count * TILE)
    )


def apply_blocks(blocks, flat_forces):
    return jnp.sum(blocks.astype(jnp.float32) * flat_forces[None], axis=1)


def sectioned_move(states, cut_lists):
    levels = cut_lists.shape[0]
    for section_no in range(levels):
        chosen = cut_lists[section_no]
        arrived = swapped(jnp.take(states, chosen, axis=0), "slab", levels - 1 - section_no)
        states = states.at[chosen].set(arrived)
    return states


def on_device(positions, forces, self_blocks, cut_lists, pair_tiles):
    fibres = positions.shape[2]
    unknowns = 3 * NODES
    flat_forces = forces.reshape(unknowns, fibres)
    states = jnp.concatenate(
        [positions.reshape(unknowns, fibres), flat_forces, apply_blocks(self_blocks, flat_forces)],
        axis=0,
    ).T
    states = sectioned_move(states, cut_lists)
    self_velocity = states[:, 2 * unknowns :].T
    tiles_count = fibres // TILE
    near = rows_to_tiles(states[:, :unknowns], tiles_count) - 0.5
    push = rows_to_tiles(states[:, unknowns : 2 * unknowns], tiles_count)
    tiles = jnp.concatenate([near, push], axis=0).transpose(1, 0, 2)
    slab_count = lax.axis_size("slab")
    bis_count = lax.axis_size("bis")
    present = pair_tiles >= 0
    safe_ids = jnp.maximum(pair_tiles, 0)
    tile_local = safe_ids % tiles_count
    relative = (safe_ids // tiles_count // slab_count - lax.axis_index("bis")) % bis_count
    extended = with_halo(tiles, (("bis", 0),), tiles_count)
    lookup = jnp.where(
        relative == 0,
        tiles_count + tile_local,
        jnp.where(relative == 1, 2 * tiles_count + tile_local, tile_local),
    )
    empty = extended.shape[0]
    lookup = jnp.where(present, lookup, empty).astype(jnp.int32)
    near, push = extended[:, :3], extended[:, 3:]
    extended = jnp.concatenate(
        [
            extended,
            jnp.sum(near * near, axis=1, keepdims=True),
            -jnp.sum(near * push, axis=1, keepdims=True),
        ],
        axis=1,
    )
    extended = jnp.pad(extended, ((0, 8), (0, 0), (0, 0)))
    extended = jnp.concatenate([extended[tiles_count : 2 * tiles_count], extended], axis=0)
    stokes_velocity = stokes_tiles(extended, jnp.where(lookup >= 0, lookup + tiles_count, 0))
    return self_velocity.reshape(3, NODES, fibres) + from_tiles(stokes_velocity, tiles_count)


def solution(mesh):
    placed = (
        P(None, None, ("bis", "slab")),
        P(None, None, ("bis", "slab")),
        P(None, None, ("bis", "slab")),
        P(None, ("bis", "slab")),
        P(None, ("bis", "slab")),
    )
    return jax.shard_map(
        on_device,
        mesh=mesh,
        in_specs=placed,
        out_specs=P(None, None, ("bis", "slab")),
        check_vma=False,
    )
```

```python
import math, functools
import jax, jax.numpy as jnp
from jax import lax
from jax.experimental import pallas as pl
from jax.experimental.pallas import tpu as pltpu
from jax.sharding import PartitionSpec as P

NODES = 32
TILE = 4
REQ = 64


def split3(x):
    h1 = x.astype(jnp.bfloat16)
    r = x - h1.astype(jnp.float32)
    h2 = r.astype(jnp.bfloat16)
    h3 = (r - h2.astype(jnp.float32)).astype(jnp.bfloat16)
    return h1, h2, h3


def dot_nn(a, b):
    return lax.dot_general(a, b, (((1,), (0,)), ((), ())), preferred_element_type=jnp.float32)


def dot_nt(a, b):
    return lax.dot_general(a, b, (((1,), (1,)), ((), ())), preferred_element_type=jnp.float32)


def pick(x, onehot):
    h1, h2, h3 = split3(x)
    return dot_nn(h1, onehot) + dot_nn(h2, onehot) + dot_nn(h3, onehot)


def spread(x, onehot):
    h1, h2, h3 = split3(x)
    return dot_nt(h1, onehot) + dot_nt(h2, onehot) + dot_nt(h3, onehot)


def flag(mask):
    return jnp.where(mask, 1.0, 0.0).astype(jnp.bfloat16)


blob_eps2 = 0.0025
stokes_scale = 1.0 / (8.0 * math.pi)


def pieces(t):
    h1 = t.astype(jnp.bfloat16).astype(jnp.float32)
    r = t - h1
    h2 = r.astype(jnp.bfloat16).astype(jnp.float32)
    h3 = (r - h2).astype(jnp.bfloat16).astype(jnp.float32)
    return h1, h2, h3


def target_features(t):
    h1, h2, h3 = pieces(t)
    row = lax.broadcasted_iota(jnp.int32, (8, 128), 0)
    zero = jnp.zeros((8, 128), jnp.float32)

    def near(h, unit):
        return jnp.where(row < 3, -2.0 * h, jnp.where(row == 6, unit, 0.0))

    def push(h, unit):
        return jnp.where(
            (row >= 3) & (row < 6), pltpu.roll(h, 3, axis=0), jnp.where(row == 7, unit, 0.0)
        )

    norm = jnp.broadcast_to(t[6:7] + blob_eps2, (8, 128))
    e1, e2, e3 = pieces(norm)
    own = jnp.where(row == 0, e1, jnp.where(row == 1, e2, jnp.where(row == 2, e3, 0.0)))
    order = [(h1, 1.0), (h1, 1.0), (h2, 0.0), (h2, 0.0), (h1, 1.0), (h3, 0.0)]
    left = jnp.concatenate([near(h, u) for h, u in order] + [own, zero], axis=0)
    right = jnp.concatenate([push(h, u) for h, u in order] + [zero, zero], axis=0)
    return jnp.concatenate([left, right], axis=1).astype(jnp.bfloat16)


def stokes_kernel(entries, look, ext, own, final, out, packed, qp0, qp1, acc0, acc1):
    count = out.shape[1]
    total = ext.shape[0]

    @pl.loop(0, total // 8)
    def _(i):
        first = pl.multiple_of(i * 8, 8)
        h1, h2, h3 = pieces(ext[pl.ds(first, 8)])
        packed[pl.ds(first, 8)] = jnp.concatenate([h1, h2, h3, h1], axis=1).astype(jnp.bfloat16)

    ones16 = jnp.ones((16, 128), jnp.bfloat16)

    def products(g, qp):
        feats = target_features(ext[g])
        for n in range(0, entries, 2):
            side = []
            for k in (n, n + 1):
                e = look[k, g]
                low = packed[e, 0:16]
                side.append(jnp.concatenate([low, low, packed[e, 16:32], ones16], axis=0))
            sources = jnp.concatenate(side, axis=1)
            qp[:, n * 128 : (n + 2) * 128] = lax.dot_general(
                feats, sources, (((0,), (0,)), ((), ())), preferred_element_type=jnp.float32
            )

    def sweep(g, qp, acc):
        ys, fs = [], []
        for n in range(entries):
            e = look[n, g]
            ys.append([jnp.broadcast_to(ext[e, i : i + 1], (8, 128)) for i in range(3)])
            fs.append([jnp.broadcast_to(ext[e, i + 3 : i + 4], (8, 128)) for i in range(3)])
        for c in range(16):
            tot = None
            for n in range(entries):
                q = qp[c * 8 : c * 8 + 8, n * 128 : n * 128 + 128]
                p = qp[128 + c * 8 : 136 + c * 8, n * 128 : n * 128 + 128]
                w = lax.rsqrt(q)
                s = p * (w * w) * w
                part = [w * fs[n][i] - s * ys[n][i] for i in range(3)] + [s]
                tot = part if tot is None else [a + b for a, b in zip(tot, part)]
            for i in range(4):
                high = tot[i].astype(jnp.bfloat16).astype(jnp.float32)
                acc[i * 128 + c * 8 : i * 128 + c * 8 + 8, 0:128] = tot[i]

    def finish(g, acc):
        a = acc[...]
        high = a.astype(jnp.bfloat16)
        low = (a - high.astype(jnp.float32)).astype(jnp.bfloat16)
        sums = lax.dot_general(
            jnp.ones((8, 256), jnp.bfloat16), jnp.concatenate([high, low], axis=1),
            (((1,), (1,)), ((), ())), preferred_element_type=jnp.float32,
        )
        t = ext[g]
        for i in range(3):
            out[i, pl.ds(g, 1)] = stokes_scale * (
                sums[0:1, i * 128 : i * 128 + 128] + t[i : i + 1] * sums[0:1, 384:512]
            )

    products(0, qp0)

    @pl.loop(0, count // 2)
    def _(h):
        g = h * 2
        products(g + 1, qp1)
        sweep(g, qp0, acc0)
        products(jnp.minimum(g + 2, count - 1), qp0)
        finish(g, acc0)
        sweep(g + 1, qp1, acc1)
        finish(g + 1, acc1)

    fibres = final.shape[1]
    back = flag(
        lax.broadcasted_iota(jnp.int32, (fibres, fibres), 0)
        == (lax.broadcasted_iota(jnp.int32, (fibres, fibres), 1) % TILE) * count
        + lax.broadcasted_iota(jnp.int32, (fibres, fibres), 1) // TILE
    )
    for c in range(3):
        turned = out[c].T
        summed = own[c * NODES : (c + 1) * NODES] + jnp.concatenate(
            [turned[t * NODES : (t + 1) * NODES] for t in range(TILE)], axis=1
        )
        final[c * NODES : (c + 1) * NODES] = pick(summed, back)


def stokes_tiles(ext, look, own):
    entries, count = look.shape
    total = ext.shape[0]
    return pl.pallas_call(
        functools.partial(stokes_kernel, entries),
        out_shape=jax.ShapeDtypeStruct(own.shape, jnp.float32),
        in_specs=[pl.BlockSpec(memory_space=pltpu.SMEM)]
        + [pl.BlockSpec(memory_space=pltpu.VMEM)] * 2,
        out_specs=pl.BlockSpec(memory_space=pltpu.VMEM),
        scratch_shapes=[
            pltpu.VMEM((3, count, 128), jnp.float32),
            pltpu.VMEM((total, 32, 128), jnp.bfloat16),
            pltpu.VMEM((256, entries * 128), jnp.float32),
            pltpu.VMEM((256, entries * 128), jnp.float32),
            pltpu.VMEM((512, 128), jnp.float32),
            pltpu.VMEM((512, 128), jnp.float32),
        ],
        compiler_params=pltpu.CompilerParams(vmem_limit_bytes=48 * 2**20),
        cost_estimate=pl.CostEstimate(flops=400_000_000, bytes_accessed=2_000_000, transcendentals=0),
    )(look, ext, own)


def exchange_kernel(
    levels, pos, force, blocks, cuts, tile_ids, ext, own_out, look_out,
    state, own, held, hots, perm, chunk, pf_out, pf_in, own_send, own_in,
    code_out, code_in, halo_out, halo_in, chunk_sem, send_sem, recv_sem,
):
    fibres = pos.shape[1]
    rows = pos.shape[0]
    count = fibres // TILE
    b, s = lax.axis_index("bis"), lax.axis_index("slab")
    nb, ns = lax.axis_size("bis"), lax.axis_size("slab")
    partners = []
    for level in range(levels):
        d = ns // 2 ** (level + 1)
        partners.append(s + d - 2 * d * ((s // d) % 2))
    right, left = (b + 1) % nb, (b + nb - 1) % nb

    barrier = pltpu.get_barrier_semaphore()
    for p in partners:
        pl.semaphore_signal(barrier, inc=1, device_id={"slab": p}, device_id_type=pl.DeviceIdType.MESH)
    for p in (right, left):
        pl.semaphore_signal(barrier, inc=1, device_id={"bis": p}, device_id_type=pl.DeviceIdType.MESH)

    depth = chunk.shape[0]
    group = chunk.shape[1]
    steps = rows // group

    def fetch(k, slot):
        return pltpu.make_async_copy(
            blocks.at[pl.ds(k * group, group)], chunk.at[slot], chunk_sem.at[slot]
        )

    for k in range(depth - 1):
        fetch(k, k).start()

    def remote(src, dst, no, where):
        return pltpu.make_async_remote_copy(
            src_ref=src, dst_ref=dst, send_sem=send_sem.at[no], recv_sem=recv_sem.at[no],
            device_id=where, device_id_type=pl.DeviceIdType.MESH,
        )

    slot_ids = lax.broadcasted_iota(jnp.int32, (fibres, cuts.shape[1]), 0)
    first_hot = flag(slot_ids == cuts[0:1, :])
    pf_out[0, 0:rows] = pick(pos[...], first_hot)
    pf_out[0, rows:] = pick(force[...], first_hot)
    pl.semaphore_wait(barrier, levels + 2)
    pf = [remote(pf_out.at[l], pf_in.at[l], l, {"slab": partners[l]}) for l in range(levels)]
    ov = [remote(own_send.at[l], own_in.at[l], levels + l, {"slab": partners[l]}) for l in range(levels)]
    pf[0].start()

    here = tile_ids[...]
    local = here % count
    rel = (here // count // ns - b + nb) % nb
    tile_rows = lax.broadcasted_iota(jnp.int32, (count, here.shape[1]), 0)
    earlier = flag(
        lax.broadcasted_iota(jnp.int32, (count, count), 0)
        < lax.broadcasted_iota(jnp.int32, (count, count), 1)
    )
    ones_row = jnp.ones((8, here.shape[1]), jnp.bfloat16)
    slots = []
    code = []
    for no, side in ((0, 1), (1, nb - 1)):
        asked = jnp.where((here >= 0) & (rel == side), local, -1)
        hot = flag(tile_rows == asked[0:1])
        named = flag(dot_nt(ones_row, hot) > 0.5)
        rank = dot_nn(named, earlier)
        slots.append(dot_nn(rank.astype(jnp.bfloat16), hot))
        code_out[no] = jnp.where(named.astype(jnp.float32) > 0.5, rank, -1.0)
        code.append(remote(
            code_out.at[no], code_in.at[no], 2 * levels + no, {"bis": right if no == 0 else left}
        ))
        code[no].start()
    look_out[...] = jnp.where(
        here < 0,
        count + 2 * REQ,
        jnp.where(
            rel == 0,
            local,
            jnp.where(
                rel == 1,
                count + slots[0].astype(jnp.int32),
                count + REQ + slots[1].astype(jnp.int32),
            ),
        ),
    )

    source_ids = lax.broadcasted_iota(jnp.int32, (fibres, count), 0)
    tile_cols = lax.broadcasted_iota(jnp.int32, (fibres, count), 1)
    for t in range(TILE):
        perm[:, t * count : (t + 1) * count] = flag(source_ids == tile_cols * TILE + t)
    state[0:rows] = pick(pos[...], perm[...])
    state[rows:] = pick(force[...], perm[...])
    for l in range(levels):
        cut = cuts[l : l + 1, :]
        hots[l] = flag(slot_ids == (cut % TILE) * count + cut // TILE)

    def self_step(k, carry):
        slot = k % depth
        fetch(k, slot).wait()

        @pl.when(k + depth - 1 < steps)
        def _():
            fetch(k + depth - 1, (k + depth - 1) % depth).start()

        made = []
        for i in range(group):
            parts = []
            for lane in range(0, fibres, 256):
                parts.append(jnp.sum(
                    chunk[slot, i, :, lane : lane + 256].astype(jnp.float32)
                    * force[:, lane : lane + 256], axis=0, keepdims=True))
            made.append(jnp.concatenate(parts, axis=1))
        own[pl.ds(pl.multiple_of(k * group, group), group)] = jnp.concatenate(made, axis=0)
        return carry

    lax.fori_loop(0, steps, self_step, 0)
    own[...] = pick(own[...], perm[...])

    def keep_mask(l):
        return dot_nt(jnp.ones((8, cuts.shape[1]), jnp.bfloat16), hots[l])[0:1] > 0.5

    def send_own(l):
        own_send[l] = pick(own[...], hots[l])
        ov[l].start()

    def take_own(l):
        ov[l].wait()
        own[...] = jnp.where(keep_mask(l), spread(own_in[l], hots[l]), own[...])

    def take_pf(l):
        pf[l].wait()
        state[...] = jnp.where(keep_mask(l), spread(pf_in[l], hots[l]), state[...])

    send_own(0)
    for l in range(levels):
        take_pf(l)
        if l + 1 < levels:
            pf_out[l + 1] = pick(state[...], hots[l + 1])
            pf[l + 1].start()
        if l > 0:
            take_own(l - 1)
            send_own(l)

    for c in range(6):
        block = jnp.concatenate(
            [state[c * NODES : (c + 1) * NODES, t * count : (t + 1) * count] for t in range(TILE)],
            axis=0,
        )
        tile = block.T
        held[:, c * 128 : (c + 1) * 128] = tile - 0.5 if c < 3 else tile

    halo = []
    rank_rows = lax.broadcasted_iota(jnp.int32, (REQ, count), 0).astype(jnp.float32)
    for no in range(2):
        code[no].wait()
        chosen = flag(code_in[no, 0:1] == rank_rows)
        halo_out[no] = dot_nn(chosen, split3(held[...])[0]) + dot_nn(
            chosen, split3(held[...])[1]) + dot_nn(chosen, split3(held[...])[2])
        halo.append(remote(
            halo_out.at[no], halo_in.at[no], 2 * levels + 2 + no, {"bis": left if no == 0 else right}
        ))
        halo[no].start()

    def lay(rows6, first, n):
        parts = [rows6[:, c * 128 : (c + 1) * 128] for c in range(6)]
        parts.append(sum(parts[i] * parts[i] for i in range(3)))
        parts.append(-sum(parts[i] * parts[i + 3] for i in range(3)))
        for c in range(8):
            ext[pl.ds(first * 8 + c, n, stride=8), :] = parts[c]

    lay(held[...], 0, count)
    ext[(count + 2 * REQ) * 8 :] = jnp.zeros((64, 128), jnp.float32)
    for no in range(2):
        halo[no].wait()
        lay(halo_in[no], count + no * REQ, REQ)
    take_own(levels - 1)
    own_out[...] = own[...]


def exchange(pos, force, blocks, cuts, tile_ids):
    rows, fibres = pos.shape
    levels, k = cuts.shape
    count = fibres // TILE
    total = count + 2 * REQ + 8
    vmem = pl.BlockSpec(memory_space=pltpu.VMEM)
    f32 = jnp.float32
    return pl.pallas_call(
        functools.partial(exchange_kernel, levels),
        out_shape=(
            jax.ShapeDtypeStruct((total * 8, 128), f32),
            jax.ShapeDtypeStruct((rows, fibres), f32),
            jax.ShapeDtypeStruct(tile_ids.shape, jnp.int32),
        ),
        in_specs=[vmem, vmem, pl.BlockSpec(memory_space=pl.ANY), vmem, vmem],
        out_specs=(vmem, vmem, vmem),
        scratch_shapes=[
            pltpu.VMEM((2 * rows, fibres), f32),
            pltpu.VMEM((rows, fibres), f32),
            pltpu.VMEM((count, 6 * 128), f32),
            pltpu.VMEM((levels, fibres, k), jnp.bfloat16),
            pltpu.VMEM((fibres, fibres), jnp.bfloat16),
            pltpu.VMEM((3, 8, rows, fibres), jnp.bfloat16),
            pltpu.VMEM((levels, 2 * rows, k), f32),
            pltpu.VMEM((levels, 2 * rows, k), f32),
            pltpu.VMEM((levels, rows, k), f32),
            pltpu.VMEM((levels, rows, k), f32),
            pltpu.VMEM((2, 8, count), f32),
            pltpu.VMEM((2, 8, count), f32),
            pltpu.VMEM((2, REQ, 6 * 128), f32),
            pltpu.VMEM((2, REQ, 6 * 128), f32),
            pltpu.SemaphoreType.DMA((3,)),
            pltpu.SemaphoreType.DMA((2 * levels + 4,)),
            pltpu.SemaphoreType.DMA((2 * levels + 4,)),
        ],
        compiler_params=pltpu.CompilerParams(
            collective_id=0, has_side_effects=True, vmem_limit_bytes=56 * 2**20
        ),
        cost_estimate=pl.CostEstimate(
            flops=400_000_000, bytes_accessed=20_000_000, transcendentals=0
        ),
    )(pos, force, blocks, cuts, tile_ids)


def on_device(positions, forces, self_blocks, cut_lists, pair_tiles):
    fibres = positions.shape[2]
    unknowns = 3 * NODES
    count = fibres // TILE
    ids = jnp.broadcast_to(pair_tiles.reshape(1, -1), (8, pair_tiles.size))
    ext, own, look = exchange(
        positions.reshape(unknowns, fibres), forces.reshape(unknowns, fibres),
        self_blocks, cut_lists, ids,
    )
    moved = stokes_tiles(
        ext.reshape(-1, 8, 128), look[0].reshape(pair_tiles.shape), own
    )
    return moved.reshape(3, NODES, fibres)


def solution(mesh):
    placed = (
        P(None, None, ("bis", "slab")),
        P(None, None, ("bis", "slab")),
        P(None, None, ("bis", "slab")),
        P(None, ("bis", "slab")),
        P(None, ("bis", "slab")),
    )
    return jax.shard_map(
        on_device,
        mesh=mesh,
        in_specs=placed,
        out_specs=P(None, None, ("bis", "slab")),
        check_vma=False,
    )
```

```python
import math, functools
import jax, jax.numpy as jnp
from jax import lax
from jax.experimental import pallas as pl
from jax.experimental.pallas import tpu as pltpu
from jax.sharding import PartitionSpec as P

NODES = 32
TILE = 4
REQ = 64


def split3(x):
    h1 = x.astype(jnp.bfloat16)
    r = x - h1.astype(jnp.float32)
    h2 = r.astype(jnp.bfloat16)
    h3 = (r - h2.astype(jnp.float32)).astype(jnp.bfloat16)
    return h1, h2, h3


def dot_nn(a, b):
    return lax.dot_general(a, b, (((1,), (0,)), ((), ())), preferred_element_type=jnp.float32)


def dot_nt(a, b):
    return lax.dot_general(a, b, (((1,), (1,)), ((), ())), preferred_element_type=jnp.float32)


def pick(x, onehot):
    h1, h2, h3 = split3(x)
    return dot_nn(h1, onehot) + dot_nn(h2, onehot) + dot_nn(h3, onehot)


def spread(x, onehot):
    h1, h2, h3 = split3(x)
    return dot_nt(h1, onehot) + dot_nt(h2, onehot) + dot_nt(h3, onehot)


def flag(mask):
    return jnp.where(mask, 1.0, 0.0).astype(jnp.bfloat16)


blob_eps2 = 0.0025
stokes_scale = 1.0 / (8.0 * math.pi)


def pieces(t):
    h1 = t.astype(jnp.bfloat16).astype(jnp.float32)
    r = t - h1
    h2 = r.astype(jnp.bfloat16).astype(jnp.float32)
    h3 = (r - h2).astype(jnp.bfloat16).astype(jnp.float32)
    return h1, h2, h3


def target_features(t):
    h1, h2, h3 = pieces(t)
    row = lax.broadcasted_iota(jnp.int32, (8, 128), 0)
    zero = jnp.zeros((8, 128), jnp.float32)

    def near(h, unit):
        return jnp.where(row < 3, -2.0 * h, jnp.where(row == 6, unit, 0.0))

    def push(h, unit):
        return jnp.where(
            (row >= 3) & (row < 6), pltpu.roll(h, 3, axis=0), jnp.where(row == 7, unit, 0.0)
        )

    norm = jnp.broadcast_to(t[6:7] + blob_eps2, (8, 128))
    e1, e2, e3 = pieces(norm)
    own = jnp.where(row == 0, e1, jnp.where(row == 1, e2, jnp.where(row == 2, e3, 0.0)))
    order = [(h1, 1.0), (h1, 1.0), (h2, 0.0), (h2, 0.0), (h1, 1.0), (h3, 0.0)]
    left = jnp.concatenate([near(h, u) for h, u in order] + [own, zero], axis=0)
    right = jnp.concatenate([push(h, u) for h, u in order] + [zero, zero], axis=0)
    return jnp.concatenate([left, right], axis=1).astype(jnp.bfloat16)


def stokes_kernel(entries, look, ext, own, final, out, packed, qp0, qp1, acc0, acc1):
    count = out.shape[1]
    total = ext.shape[0]

    @pl.loop(0, total // 8)
    def _(i):
        first = pl.multiple_of(i * 8, 8)
        h1, h2, h3 = pieces(ext[pl.ds(first, 8)])
        packed[pl.ds(first, 8)] = jnp.concatenate([h1, h2, h3, h1], axis=1).astype(jnp.bfloat16)

    ones16 = jnp.ones((16, 128), jnp.bfloat16)

    def products(g, qp):
        feats = target_features(ext[g])
        for n in range(0, entries, 2):
            side = []
            for k in (n, n + 1):
                e = look[k, g]
                low = packed[e, 0:16]
                side.append(jnp.concatenate([low, low, packed[e, 16:32], ones16], axis=0))
            sources = jnp.concatenate(side, axis=1)
            qp[:, n * 128 : (n + 2) * 128] = lax.dot_general(
                feats, sources, (((0,), (0,)), ((), ())), preferred_element_type=jnp.float32
            )

    def sweep(g, qp, acc):
        ys, fs = [], []
        for n in range(entries):
            e = look[n, g]
            ys.append([jnp.broadcast_to(ext[e, i : i + 1], (8, 128)) for i in range(3)])
            fs.append([jnp.broadcast_to(ext[e, i + 3 : i + 4], (8, 128)) for i in range(3)])
        for c in range(16):
            tot = None
            for n in range(entries):
                q = qp[c * 8 : c * 8 + 8, n * 128 : n * 128 + 128]
                p = qp[128 + c * 8 : 136 + c * 8, n * 128 : n * 128 + 128]
                w = lax.rsqrt(q)
                s = p * (w * w) * w
                part = [w * fs[n][i] - s * ys[n][i] for i in range(3)] + [s]
                tot = part if tot is None else [a + b for a, b in zip(tot, part)]
            for i in range(4):
                acc[i * 128 + c * 8 : i * 128 + c * 8 + 8, 0:128] = tot[i]

    def finish(g, acc):
        sums = [jnp.sum(acc[i*128:i*128+128].T, axis=0, keepdims=True) for i in range(4)]
        t = ext[g]
        for i in range(3):
            out[i, pl.ds(g, 1)] = stokes_scale * (
                sums[i] + t[i : i + 1] * sums[3]
            )

    products(0, qp0)

    @pl.loop(0, count // 2)
    def _(h):
        g = h * 2
        finish(jnp.maximum(g - 1, 0), acc1)
        products(g + 1, qp1)
        sweep(g, qp0, acc0)
        finish(g, acc0)
        products(jnp.minimum(g + 2, count - 1), qp0)
        sweep(g + 1, qp1, acc1)

    finish(count - 1, acc1)

    fibres = final.shape[1]
    back = flag(
        lax.broadcasted_iota(jnp.int32, (fibres, fibres), 0)
        == (lax.broadcasted_iota(jnp.int32, (fibres, fibres), 1) % TILE) * count
        + lax.broadcasted_iota(jnp.int32, (fibres, fibres), 1) // TILE
    )
    for c in range(3):
        turned = out[c].T
        summed = own[c * NODES : (c + 1) * NODES] + jnp.concatenate(
            [turned[t * NODES : (t + 1) * NODES] for t in range(TILE)], axis=1
        )
        final[c * NODES : (c + 1) * NODES] = pick(summed, back)


def stokes_tiles(ext, look, own):
    entries, count = look.shape
    total = ext.shape[0]
    return pl.pallas_call(
        functools.partial(stokes_kernel, entries),
        out_shape=jax.ShapeDtypeStruct(own.shape, jnp.float32),
        in_specs=[pl.BlockSpec(memory_space=pltpu.SMEM)]
        + [pl.BlockSpec(memory_space=pltpu.VMEM)] * 2,
        out_specs=pl.BlockSpec(memory_space=pltpu.VMEM),
        scratch_shapes=[
            pltpu.VMEM((3, count, 128), jnp.float32),
            pltpu.VMEM((total, 32, 128), jnp.bfloat16),
            pltpu.VMEM((256, entries * 128), jnp.float32),
            pltpu.VMEM((256, entries * 128), jnp.float32),
            pltpu.VMEM((512, 128), jnp.float32),
            pltpu.VMEM((512, 128), jnp.float32),
        ],
        compiler_params=pltpu.CompilerParams(vmem_limit_bytes=48 * 2**20),
        cost_estimate=pl.CostEstimate(flops=400_000_000, bytes_accessed=2_000_000, transcendentals=0),
    )(look, ext, own)


def exchange_kernel(
    levels, pos, force, blocks, cuts, tile_ids, ext, own_out, look_out,
    state, own, held, hots, perm, chunk, pf_out, pf_in, own_send, own_in,
    code_out, code_in, halo_out, halo_in, chunk_sem, send_sem, recv_sem,
):
    fibres = pos.shape[1]
    rows = pos.shape[0]
    count = fibres // TILE
    b, s = lax.axis_index("bis"), lax.axis_index("slab")
    nb, ns = lax.axis_size("bis"), lax.axis_size("slab")
    partners = []
    for level in range(levels):
        d = ns // 2 ** (level + 1)
        partners.append(s + d - 2 * d * ((s // d) % 2))
    right, left = (b + 1) % nb, (b + nb - 1) % nb

    barrier = pltpu.get_barrier_semaphore()
    for p in partners:
        pl.semaphore_signal(barrier, inc=1, device_id={"slab": p}, device_id_type=pl.DeviceIdType.MESH)
    for p in (right, left):
        pl.semaphore_signal(barrier, inc=1, device_id={"bis": p}, device_id_type=pl.DeviceIdType.MESH)

    depth = chunk.shape[0]
    group = chunk.shape[1]
    steps = rows // group

    def fetch(k, slot):
        return pltpu.make_async_copy(
            blocks.at[pl.ds(k * group, group)], chunk.at[slot], chunk_sem.at[slot]
        )

    for k in range(depth - 1):
        fetch(k, k).start()

    def remote(src, dst, no, where):
        return pltpu.make_async_remote_copy(
            src_ref=src, dst_ref=dst, send_sem=send_sem.at[no], recv_sem=recv_sem.at[no],
            device_id=where, device_id_type=pl.DeviceIdType.MESH,
        )

    slot_ids = lax.broadcasted_iota(jnp.int32, (fibres, cuts.shape[1]), 0)
    first_hot = flag(slot_ids == cuts[0:1, :])
    pf_out[0, 0:rows] = pick(pos[...], first_hot)
    pf_out[0, rows:] = pick(force[...], first_hot)
    pl.semaphore_wait(barrier, levels + 2)
    pf = [remote(pf_out.at[l], pf_in.at[l], l, {"slab": partners[l]}) for l in range(levels)]
    ov = [remote(own_send.at[l], own_in.at[l], levels + l, {"slab": partners[l]}) for l in range(levels)]
    pf[0].start()

    here = tile_ids[...]
    local = here % count
    rel = (here // count // ns - b + nb) % nb
    tile_rows = lax.broadcasted_iota(jnp.int32, (count, here.shape[1]), 0)
    earlier = flag(
        lax.broadcasted_iota(jnp.int32, (count, count), 0)
        < lax.broadcasted_iota(jnp.int32, (count, count), 1)
    )
    ones_row = jnp.ones((8, here.shape[1]), jnp.bfloat16)
    slots = []
    code = []
    for no, side in ((0, 1), (1, nb - 1)):
        asked = jnp.where((here >= 0) & (rel == side), local, -1)
        hot = flag(tile_rows == asked[0:1])
        named = flag(dot_nt(ones_row, hot) > 0.5)
        rank = dot_nn(named, earlier)
        slots.append(dot_nn(rank.astype(jnp.bfloat16), hot))
        code_out[no] = jnp.where(named.astype(jnp.float32) > 0.5, rank, -1.0)
        code.append(remote(
            code_out.at[no], code_in.at[no], 2 * levels + no, {"bis": right if no == 0 else left}
        ))
        code[no].start()
    look_out[...] = jnp.where(
        here < 0,
        count + 2 * REQ,
        jnp.where(
            rel == 0,
            local,
            jnp.where(
                rel == 1,
                count + slots[0].astype(jnp.int32),
                count + REQ + slots[1].astype(jnp.int32),
            ),
        ),
    )

    source_ids = lax.broadcasted_iota(jnp.int32, (fibres, count), 0)
    tile_cols = lax.broadcasted_iota(jnp.int32, (fibres, count), 1)
    for t in range(TILE):
        perm[:, t * count : (t + 1) * count] = flag(source_ids == tile_cols * TILE + t)
    state[0:rows] = pick(pos[...], perm[...])
    state[rows:] = pick(force[...], perm[...])
    for l in range(levels):
        cut = cuts[l : l + 1, :]
        hots[l] = flag(slot_ids == (cut % TILE) * count + cut // TILE)

    def self_step(k, carry):
        slot = k % depth
        fetch(k, slot).wait()

        @pl.when(k + depth - 1 < steps)
        def _():
            fetch(k + depth - 1, (k + depth - 1) % depth).start()

        made = []
        for i in range(group):
            parts = []
            for lane in range(0, fibres, 256):
                parts.append(jnp.sum(
                    chunk[slot, i, :, lane : lane + 256].astype(jnp.float32)
                    * force[:, lane : lane + 256], axis=0, keepdims=True))
            made.append(jnp.concatenate(parts, axis=1))
        own[pl.ds(pl.multiple_of(k * group, group), group)] = jnp.concatenate(made, axis=0)
        return carry

    lax.fori_loop(0, steps, self_step, 0)
    own[...] = pick(own[...], perm[...])

    def keep_mask(l):
        return dot_nt(jnp.ones((8, cuts.shape[1]), jnp.bfloat16), hots[l])[0:1] > 0.5

    def send_own(l):
        own_send[l] = pick(own[...], hots[l])
        ov[l].start()

    def take_own(l):
        ov[l].wait()
        own[...] = jnp.where(keep_mask(l), spread(own_in[l], hots[l]), own[...])

    def take_pf(l):
        pf[l].wait()
        state[...] = jnp.where(keep_mask(l), spread(pf_in[l], hots[l]), state[...])

    send_own(0)
    for l in range(levels):
        take_pf(l)
        if l + 1 < levels:
            pf_out[l + 1] = pick(state[...], hots[l + 1])
            pf[l + 1].start()
        if l > 0:
            take_own(l - 1)
            send_own(l)

    for c in range(6):
        block = jnp.concatenate(
            [state[c * NODES : (c + 1) * NODES, t * count : (t + 1) * count] for t in range(TILE)],
            axis=0,
        )
        tile = block.T
        held[:, c * 128 : (c + 1) * 128] = tile - 0.5 if c < 3 else tile

    halo = []
    rank_rows = lax.broadcasted_iota(jnp.int32, (REQ, count), 0).astype(jnp.float32)
    for no in range(2):
        code[no].wait()
        chosen = flag(code_in[no, 0:1] == rank_rows)
        halo_out[no] = dot_nn(chosen, split3(held[...])[0]) + dot_nn(
            chosen, split3(held[...])[1]) + dot_nn(chosen, split3(held[...])[2])
        halo.append(remote(
            halo_out.at[no], halo_in.at[no], 2 * levels + 2 + no, {"bis": left if no == 0 else right}
        ))
        halo[no].start()

    def lay(rows6, first, n):
        parts = [rows6[:, c * 128 : (c + 1) * 128] for c in range(6)]
        parts.append(sum(parts[i] * parts[i] for i in range(3)))
        parts.append(-sum(parts[i] * parts[i + 3] for i in range(3)))
        for c in range(8):
            ext[pl.ds(first * 8 + c, n, stride=8), :] = parts[c]

    lay(held[...], 0, count)
    ext[(count + 2 * REQ) * 8 :] = jnp.zeros((64, 128), jnp.float32)
    for no in range(2):
        halo[no].wait()
        lay(halo_in[no], count + no * REQ, REQ)
    take_own(levels - 1)
    own_out[...] = own[...]


def exchange(pos, force, blocks, cuts, tile_ids):
    rows, fibres = pos.shape
    levels, k = cuts.shape
    count = fibres // TILE
    total = count + 2 * REQ + 8
    vmem = pl.BlockSpec(memory_space=pltpu.VMEM)
    f32 = jnp.float32
    return pl.pallas_call(
        functools.partial(exchange_kernel, levels),
        out_shape=(
            jax.ShapeDtypeStruct((total * 8, 128), f32),
            jax.ShapeDtypeStruct((rows, fibres), f32),
            jax.ShapeDtypeStruct(tile_ids.shape, jnp.int32),
        ),
        in_specs=[vmem, vmem, pl.BlockSpec(memory_space=pl.ANY), vmem, vmem],
        out_specs=(vmem, vmem, vmem),
        scratch_shapes=[
            pltpu.VMEM((2 * rows, fibres), f32),
            pltpu.VMEM((rows, fibres), f32),
            pltpu.VMEM((count, 6 * 128), f32),
            pltpu.VMEM((levels, fibres, k), jnp.bfloat16),
            pltpu.VMEM((fibres, fibres), jnp.bfloat16),
            pltpu.VMEM((3, 8, rows, fibres), jnp.bfloat16),
            pltpu.VMEM((levels, 2 * rows, k), f32),
            pltpu.VMEM((levels, 2 * rows, k), f32),
            pltpu.VMEM((levels, rows, k), f32),
            pltpu.VMEM((levels, rows, k), f32),
            pltpu.VMEM((2, 8, count), f32),
            pltpu.VMEM((2, 8, count), f32),
            pltpu.VMEM((2, REQ, 6 * 128), f32),
            pltpu.VMEM((2, REQ, 6 * 128), f32),
            pltpu.SemaphoreType.DMA((3,)),
            pltpu.SemaphoreType.DMA((2 * levels + 4,)),
            pltpu.SemaphoreType.DMA((2 * levels + 4,)),
        ],
        compiler_params=pltpu.CompilerParams(
            collective_id=0, has_side_effects=True, vmem_limit_bytes=56 * 2**20
        ),
        cost_estimate=pl.CostEstimate(
            flops=400_000_000, bytes_accessed=20_000_000, transcendentals=0
        ),
    )(pos, force, blocks, cuts, tile_ids)


def on_device(positions, forces, self_blocks, cut_lists, pair_tiles):
    fibres = positions.shape[2]
    unknowns = 3 * NODES
    count = fibres // TILE
    ids = jnp.broadcast_to(pair_tiles.reshape(1, -1), (8, pair_tiles.size))
    ext, own, look = exchange(
        positions.reshape(unknowns, fibres), forces.reshape(unknowns, fibres),
        self_blocks, cut_lists, ids,
    )
    moved = stokes_tiles(
        ext.reshape(-1, 8, 128), look[0].reshape(pair_tiles.shape), own
    )
    return moved.reshape(3, NODES, fibres)


def solution(mesh):
    placed = (
        P(None, None, ("bis", "slab")),
        P(None, None, ("bis", "slab")),
        P(None, None, ("bis", "slab")),
        P(None, ("bis", "slab")),
        P(None, ("bis", "slab")),
    )
    return jax.shard_map(
        on_device,
        mesh=mesh,
        in_specs=placed,
        out_specs=P(None, None, ("bis", "slab")),
        check_vma=False,
    )
```

```python
import math, functools
import jax, jax.numpy as jnp
from jax import lax
from jax.experimental import pallas as pl
from jax.experimental.pallas import tpu as pltpu
from jax.sharding import PartitionSpec as P

NODES = 32
TILE = 4
REQ = 64


def split3(x):
    h1 = x.astype(jnp.bfloat16)
    r = x - h1.astype(jnp.float32)
    h2 = r.astype(jnp.bfloat16)
    h3 = (r - h2.astype(jnp.float32)).astype(jnp.bfloat16)
    return h1, h2, h3


def dot_nn(a, b):
    return lax.dot_general(a, b, (((1,), (0,)), ((), ())), preferred_element_type=jnp.float32)


def dot_nt(a, b):
    return lax.dot_general(a, b, (((1,), (1,)), ((), ())), preferred_element_type=jnp.float32)


def pick(x, onehot):
    h1, h2, h3 = split3(x)
    return dot_nn(h1, onehot) + dot_nn(h2, onehot) + dot_nn(h3, onehot)


def spread(x, onehot):
    h1, h2, h3 = split3(x)
    return dot_nt(h1, onehot) + dot_nt(h2, onehot) + dot_nt(h3, onehot)


def flag(mask):
    return jnp.where(mask, 1.0, 0.0).astype(jnp.bfloat16)


blob_eps2 = 0.0025
stokes_scale = 1.0 / (8.0 * math.pi)


def pieces(t):
    h1 = t.astype(jnp.bfloat16).astype(jnp.float32)
    r = t - h1
    h2 = r.astype(jnp.bfloat16).astype(jnp.float32)
    h3 = (r - h2).astype(jnp.bfloat16).astype(jnp.float32)
    return h1, h2, h3


def target_features(t):
    h1, h2, h3 = pieces(t)
    row = lax.broadcasted_iota(jnp.int32, (8, 128), 0)
    zero = jnp.zeros((8, 128), jnp.float32)

    def near(h, unit):
        return jnp.where(row < 3, -2.0 * h, jnp.where(row == 6, unit, 0.0))

    def push(h, unit):
        return jnp.where(
            (row >= 3) & (row < 6), pltpu.roll(h, 3, axis=0), jnp.where(row == 7, unit, 0.0)
        )

    norm = jnp.broadcast_to(t[6:7] + blob_eps2, (8, 128))
    e1, e2, e3 = pieces(norm)
    own = jnp.where(row == 0, e1, jnp.where(row == 1, e2, jnp.where(row == 2, e3, 0.0)))
    order = [(h1, 1.0), (h1, 1.0), (h2, 0.0), (h2, 0.0), (h1, 1.0), (h3, 0.0)]
    left = jnp.concatenate([near(h, u) for h, u in order] + [own, zero], axis=0)
    right = jnp.concatenate([push(h, u) for h, u in order] + [zero, zero], axis=0)
    return jnp.concatenate([left, right], axis=1).astype(jnp.bfloat16)


def stokes_kernel(entries, look, ext, own, final, out, packed, qp0, qp1, acc0, acc1):
    count = out.shape[1]
    total = ext.shape[0]

    @pl.loop(0, total // 8)
    def _(i):
        first = pl.multiple_of(i * 8, 8)
        h1, h2, h3 = pieces(ext[pl.ds(first, 8)])
        packed[pl.ds(first, 8)] = jnp.concatenate([h1, h2, h3, h1], axis=1).astype(jnp.bfloat16)

    ones16 = jnp.ones((16, 128), jnp.bfloat16)

    def products(g, qp):
        feats = target_features(ext[g])
        for n in range(0, entries, 2):
            side = []
            for k in (n, n + 1):
                e = look[k, g]
                low = packed[e, 0:16]
                side.append(jnp.concatenate([low, low, packed[e, 16:32], ones16], axis=0))
            sources = jnp.concatenate(side, axis=1)
            qp[:, n * 128 : (n + 2) * 128] = lax.dot_general(
                feats, sources, (((0,), (0,)), ((), ())), preferred_element_type=jnp.float32
            )

    def sweep(g, qp, acc):
        ys, fs = [], []
        for n in range(entries):
            e = look[n, g]
            ys.append([jnp.broadcast_to(ext[e, i : i + 1], (8, 128)) for i in range(3)])
            fs.append([jnp.broadcast_to(ext[e, i + 3 : i + 4], (8, 128)) for i in range(3)])
        for c in range(16):
            tot = None
            for n in range(entries):
                q = qp[c * 8 : c * 8 + 8, n * 128 : n * 128 + 128]
                p = qp[128 + c * 8 : 136 + c * 8, n * 128 : n * 128 + 128]
                w = lax.rsqrt(q)
                s = p * (w * w) * w
                part = [w * fs[n][i] - s * ys[n][i] for i in range(3)] + [s]
                tot = part if tot is None else [a + b for a, b in zip(tot, part)]
            for i in range(4):
                acc[i * 128 + c * 8 : i * 128 + c * 8 + 8, 0:128] = tot[i]

    def finish(g, acc):
        sums = [jnp.sum(acc[i*128:i*128+128].T, axis=0, keepdims=True) for i in range(4)]
        t = ext[g]
        for i in range(3):
            out[i, pl.ds(g, 1)] = stokes_scale * (
                sums[i] + t[i : i + 1] * sums[3]
            )

    products(0, qp0)

    @pl.loop(0, count // 2)
    def _(h):
        g = h * 2
        finish(jnp.maximum(g - 1, 0), acc1)
        products(g + 1, qp1)
        sweep(g, qp0, acc0)
        finish(g, acc0)
        products(jnp.minimum(g + 2, count - 1), qp0)
        sweep(g + 1, qp1, acc1)

    finish(count - 1, acc1)

    fibres = final.shape[1]
    back = flag(
        lax.broadcasted_iota(jnp.int32, (fibres, fibres), 0)
        == (lax.broadcasted_iota(jnp.int32, (fibres, fibres), 1) % TILE) * count
        + lax.broadcasted_iota(jnp.int32, (fibres, fibres), 1) // TILE
    )
    for c in range(3):
        turned = out[c].T
        summed = own[c * NODES : (c + 1) * NODES] + jnp.concatenate(
            [turned[t * NODES : (t + 1) * NODES] for t in range(TILE)], axis=1
        )
        final[c * NODES : (c + 1) * NODES] = pick(summed, back)


def stokes_tiles(ext, look, own):
    entries, count = look.shape
    total = ext.shape[0]
    return pl.pallas_call(
        functools.partial(stokes_kernel, entries),
        out_shape=jax.ShapeDtypeStruct(own.shape, jnp.float32),
        in_specs=[pl.BlockSpec(memory_space=pltpu.SMEM)]
        + [pl.BlockSpec(memory_space=pltpu.VMEM)] * 2,
        out_specs=pl.BlockSpec(memory_space=pltpu.VMEM),
        scratch_shapes=[
            pltpu.VMEM((3, count, 128), jnp.float32),
            pltpu.VMEM((total, 32, 128), jnp.bfloat16),
            pltpu.VMEM((256, entries * 128), jnp.float32),
            pltpu.VMEM((256, entries * 128), jnp.float32),
            pltpu.VMEM((512, 128), jnp.float32),
            pltpu.VMEM((512, 128), jnp.float32),
        ],
        compiler_params=pltpu.CompilerParams(vmem_limit_bytes=48 * 2**20),
        cost_estimate=pl.CostEstimate(flops=400_000_000, bytes_accessed=2_000_000, transcendentals=0),
    )(look, ext, own)


def exchange_kernel(
    levels, pos, force, blocks, cuts, tile_ids, ext, own_out, look_out,
    state, own, held, hots, perm, chunk, pf_out, pf_in, own_send, own_in,
    code_out, code_in, halo_out, halo_in, chunk_sem, send_sem, recv_sem,
):
    fibres = pos.shape[1]
    rows = pos.shape[0]
    count = fibres // TILE
    b, s = lax.axis_index("bis"), lax.axis_index("slab")
    nb, ns = lax.axis_size("bis"), lax.axis_size("slab")
    partners = []
    for level in range(levels):
        d = ns // 2 ** (level + 1)
        partners.append(s + d - 2 * d * ((s // d) % 2))
    right, left = (b + 1) % nb, (b + nb - 1) % nb

    barrier = pltpu.get_barrier_semaphore()
    for p in partners:
        pl.semaphore_signal(barrier, inc=1, device_id={"slab": p}, device_id_type=pl.DeviceIdType.MESH)
    for p in (right, left):
        pl.semaphore_signal(barrier, inc=1, device_id={"bis": p}, device_id_type=pl.DeviceIdType.MESH)

    depth = chunk.shape[0]
    group = chunk.shape[1]
    steps = rows // group

    def fetch(k, slot):
        return pltpu.make_async_copy(
            blocks.at[pl.ds(k * group, group)], chunk.at[slot], chunk_sem.at[slot]
        )

    for k in range(depth - 1):
        fetch(k, k).start()

    def remote(src, dst, no, where):
        return pltpu.make_async_remote_copy(
            src_ref=src, dst_ref=dst, send_sem=send_sem.at[no], recv_sem=recv_sem.at[no],
            device_id=where, device_id_type=pl.DeviceIdType.MESH,
        )

    slot_ids = lax.broadcasted_iota(jnp.int32, (fibres, cuts.shape[1]), 0)
    first_hot = flag(slot_ids == cuts[0:1, :])
    pf_out[0, 0:rows] = pick(pos[...], first_hot)
    pf_out[0, rows:] = pick(force[...], first_hot)
    pl.semaphore_wait(barrier, levels + 2)
    pf = [remote(pf_out.at[l], pf_in.at[l], l, {"slab": partners[l]}) for l in range(levels)]
    ov = [remote(own_send.at[l], own_in.at[l], levels + l, {"slab": partners[l]}) for l in range(levels)]
    pf[0].start()

    here = tile_ids[...]
    local = here % count
    rel = (here // count // ns - b + nb) % nb
    tile_rows = lax.broadcasted_iota(jnp.int32, (count, here.shape[1]), 0)
    earlier = flag(
        lax.broadcasted_iota(jnp.int32, (count, count), 0)
        < lax.broadcasted_iota(jnp.int32, (count, count), 1)
    )
    ones_row = jnp.ones((8, here.shape[1]), jnp.bfloat16)
    slots = []
    code = []
    for no, side in ((0, 1), (1, nb - 1)):
        asked = jnp.where((here >= 0) & (rel == side), local, -1)
        hot = flag(tile_rows == asked[0:1])
        named = flag(dot_nt(ones_row, hot) > 0.5)
        rank = dot_nn(named, earlier)
        slots.append(dot_nn(rank.astype(jnp.bfloat16), hot))
        code_out[no] = jnp.where(named.astype(jnp.float32) > 0.5, rank, -1.0)
        code.append(remote(
            code_out.at[no], code_in.at[no], 2 * levels + no, {"bis": right if no == 0 else left}
        ))
        code[no].start()
    look_out[...] = jnp.where(
        here < 0,
        count + 2 * REQ,
        jnp.where(
            rel == 0,
            local,
            jnp.where(
                rel == 1,
                count + slots[0].astype(jnp.int32),
                count + REQ + slots[1].astype(jnp.int32),
            ),
        ),
    )

    source_ids = lax.broadcasted_iota(jnp.int32, (fibres, count), 0)
    tile_cols = lax.broadcasted_iota(jnp.int32, (fibres, count), 1)
    for t in range(TILE):
        perm[:, t * count : (t + 1) * count] = flag(source_ids == tile_cols * TILE + t)
    state[0:rows] = pick(pos[...], perm[...])
    state[rows:] = pick(force[...], perm[...])
    for l in range(levels):
        cut = cuts[l : l + 1, :]
        hots[l] = flag(slot_ids == (cut % TILE) * count + cut // TILE)

    def self_step(k, carry):
        slot = k % depth
        fetch(k, slot).wait()

        @pl.when(k + depth - 1 < steps)
        def _():
            fetch(k + depth - 1, (k + depth - 1) % depth).start()

        made = []
        for i in range(group):
            parts = []
            for lane in range(0, fibres, 256):
                parts.append(jnp.sum(
                    chunk[slot, i, :, lane : lane + 256].astype(jnp.float32)
                    * force[:, lane : lane + 256], axis=0, keepdims=True))
            made.append(jnp.concatenate(parts, axis=1))
        own[pl.ds(pl.multiple_of(k * group, group), group)] = jnp.concatenate(made, axis=0)
        return carry

    lax.fori_loop(0, steps, self_step, 0)
    own[...] = pick(own[...], perm[...])

    def keep_mask(l):
        return dot_nt(jnp.ones((8, cuts.shape[1]), jnp.bfloat16), hots[l])[0:1] > 0.5

    def send_own(l):
        own_send[l] = pick(own[...], hots[l])
        ov[l].start()

    def take_own(l):
        ov[l].wait()
        own[...] = jnp.where(keep_mask(l), spread(own_in[l], hots[l]), own[...])

    def take_pf(l):
        pf[l].wait()
        state[...] = jnp.where(keep_mask(l), spread(pf_in[l], hots[l]), state[...])

    send_own(0)
    for l in range(levels):
        take_pf(l)
        if l + 1 < levels:
            pf_out[l + 1] = pick(state[...], hots[l + 1])
            pf[l + 1].start()
        if l > 0:
            take_own(l - 1)
            send_own(l)

    for c in range(6):
        block = jnp.concatenate(
            [state[c * NODES : (c + 1) * NODES, t * count : (t + 1) * count] for t in range(TILE)],
            axis=0,
        )
        tile = block.T
        held[:, c * 128 : (c + 1) * 128] = tile - 0.5 if c < 3 else tile

    halo = []
    tile_parts = split3(held[...])
    rank_rows = lax.broadcasted_iota(jnp.int32, (REQ, count), 0).astype(jnp.float32)
    for no in range(2):
        code[no].wait()
        chosen = flag(code_in[no, 0:1] == rank_rows)
        halo_out[no] = (
            dot_nn(chosen, tile_parts[0])
            + dot_nn(chosen, tile_parts[1])
            + dot_nn(chosen, tile_parts[2])
        )
        halo.append(remote(
            halo_out.at[no], halo_in.at[no], 2 * levels + 2 + no, {"bis": left if no == 0 else right}
        ))
        halo[no].start()

    def lay(rows6, first, n):
        parts = [rows6[:, c * 128 : (c + 1) * 128] for c in range(6)]
        parts.append(sum(parts[i] * parts[i] for i in range(3)))
        parts.append(-sum(parts[i] * parts[i + 3] for i in range(3)))
        for c in range(8):
            ext[pl.ds(first * 8 + c, n, stride=8), :] = parts[c]

    lay(held[...], 0, count)
    ext[(count + 2 * REQ) * 8 :] = jnp.zeros((64, 128), jnp.float32)
    for no in range(2):
        halo[no].wait()
        lay(halo_in[no], count + no * REQ, REQ)
    take_own(levels - 1)
    own_out[...] = own[...]


def exchange(pos, force, blocks, cuts, tile_ids):
    rows, fibres = pos.shape
    levels, k = cuts.shape
    count = fibres // TILE
    total = count + 2 * REQ + 8
    vmem = pl.BlockSpec(memory_space=pltpu.VMEM)
    f32 = jnp.float32
    return pl.pallas_call(
        functools.partial(exchange_kernel, levels),
        out_shape=(
            jax.ShapeDtypeStruct((total * 8, 128), f32),
            jax.ShapeDtypeStruct((rows, fibres), f32),
            jax.ShapeDtypeStruct(tile_ids.shape, jnp.int32),
        ),
        in_specs=[vmem, vmem, pl.BlockSpec(memory_space=pl.ANY), vmem, vmem],
        out_specs=(vmem, vmem, vmem),
        scratch_shapes=[
            pltpu.VMEM((2 * rows, fibres), f32),
            pltpu.VMEM((rows, fibres), f32),
            pltpu.VMEM((count, 6 * 128), f32),
            pltpu.VMEM((levels, fibres, k), jnp.bfloat16),
            pltpu.VMEM((fibres, fibres), jnp.bfloat16),
            pltpu.VMEM((3, 8, rows, fibres), jnp.bfloat16),
            pltpu.VMEM((levels, 2 * rows, k), f32),
            pltpu.VMEM((levels, 2 * rows, k), f32),
            pltpu.VMEM((levels, rows, k), f32),
            pltpu.VMEM((levels, rows, k), f32),
            pltpu.VMEM((2, 8, count), f32),
            pltpu.VMEM((2, 8, count), f32),
            pltpu.VMEM((2, REQ, 6 * 128), f32),
            pltpu.VMEM((2, REQ, 6 * 128), f32),
            pltpu.SemaphoreType.DMA((3,)),
            pltpu.SemaphoreType.DMA((2 * levels + 4,)),
            pltpu.SemaphoreType.DMA((2 * levels + 4,)),
        ],
        compiler_params=pltpu.CompilerParams(
            collective_id=0, has_side_effects=True, vmem_limit_bytes=56 * 2**20
        ),
        cost_estimate=pl.CostEstimate(
            flops=400_000_000, bytes_accessed=20_000_000, transcendentals=0
        ),
    )(pos, force, blocks, cuts, tile_ids)


def on_device(positions, forces, self_blocks, cut_lists, pair_tiles):
    fibres = positions.shape[2]
    unknowns = 3 * NODES
    count = fibres // TILE
    ids = jnp.broadcast_to(pair_tiles.reshape(1, -1), (8, pair_tiles.size))
    ext, own, look = exchange(
        positions.reshape(unknowns, fibres), forces.reshape(unknowns, fibres),
        self_blocks, cut_lists, ids,
    )
    moved = stokes_tiles(
        ext.reshape(-1, 8, 128), look[0].reshape(pair_tiles.shape), own
    )
    return moved.reshape(3, NODES, fibres)


def solution(mesh):
    placed = (
        P(None, None, ("bis", "slab")),
        P(None, None, ("bis", "slab")),
        P(None, None, ("bis", "slab")),
        P(None, ("bis", "slab")),
        P(None, ("bis", "slab")),
    )
    return jax.shard_map(
        on_device,
        mesh=mesh,
        in_specs=placed,
        out_specs=P(None, None, ("bis", "slab")),
        check_vma=False,
    )
```
